512 devices in a mesh: row: 32 (over z_hi, y, core), chan: 16 (over z_lo, x).
Axes of the slice: x: 4, y: 4, z: 16 (z_hi: 4, z_lo: 4; z = z_hi * 4 + z_lo), core: 2. Of those that a mesh axis runs over, the one named last changes fastest.
Arguments:
- features: bfloat16 [1, 256, 256, 256], P(None, 'chan', 'row'), may hold values from -6 to 6
- pre_act: bfloat16 [1, 512, 128, 128], P(None, 'chan', 'row'), may hold values from -6 to 6
- cotangent: bfloat16 [1, 512, 128, 128], P(None, 'chan', 'row'), may hold values from -6 to 6
- w_strided: bfloat16 [4, 4, 256, 512], P(None, None, 'chan'), may hold values from -0.09375 to 0.09375
- w_square: bfloat16 [3, 3, 512, 512], P(None, None, 'chan'), may hold values from -0.09375 to 0.09375
Outputs:
- grad_features: bfloat16 [1, 256, 256, 256], P(None, 'chan', 'row')
- grad_w_strided: float32 [4, 4, 256, 512], P(None, None, 'chan', 'row')
- grad_w_square: float32 [3, 3, 512, 512], P(None, None, 'chan', 'row')
The draws below stay inside these ranges and needn't reach their ends.
All inputs are finite; a program needn't handle non-finite values.
Results may differ from the reference program's by a relative error of at most 0.0049.
Values may be sent and summed in bfloat16 or wider, within the bound.
A program may use at most 64 MiB of HBM per device.

```python
import math
import jax
import jax.numpy as jnp
from jax import lax

BATCH = 1
WIDTH = 256
CIN = 256
C = 512
OH = 128
H = 256
OW = 128


def spiked(result, stream_key, source, target, blocks, factor):
    owner, partner = [(jnp.arange(result.shape[position]) // (result.shape[position] // blocks)).reshape([-1 if axis == position else 1 for axis in range(result.ndim)]) for position in (source, target)]
    chosen = jax.random.permutation(stream_key, blocks)[partner]
    strong = (owner == chosen) | (owner == (partner + blocks // 2) % blocks)
    return jnp.where(strong, factor * result, result)


def level_of(own_key, dims, split, least, top_value):
    def one(position, parts):
        steps = jax.random.uniform(jax.random.fold_in(jax.random.fold_in(own_key, 6), position), (parts,), jnp.float32, least / len(split), top_value / len(split))
        return jnp.repeat(jnp.exp(steps), dims[position] // parts).reshape((-1,) + (1,) * (len(dims) - position - 1))

    loudness = one(*split[0])
    for cut in split[1:]:
        loudness = loudness * one(*cut)
    return loudness


def noise(key, dims, spread, reach, pieces=(), kind=jnp.bfloat16):
    result = spread * jax.random.normal(key, dims, jnp.float32)
    if pieces:
        result = result * level_of(key, dims, pieces, -0.22, 0.18)
    return jnp.clip(result, -reach, reach).astype(kind)


def noise_with(own_key, shape, scale, bound, pieces, heavy, dtype=jnp.bfloat16):
    drawn = scale * jax.random.normal(own_key, shape, jnp.float32)
    if pieces:
        drawn = drawn * level_of(own_key, shape, pieces, -0.22, 0.18)
    return jnp.clip(spiked(drawn, jax.random.fold_in(own_key, 3), *heavy), -bound, bound).astype(dtype)


def setup_inputs(seed: int = 0) -> dict:
    arg_keys = jax.random.split(jax.random.key(seed), 6)
    features = noise(arg_keys[0], (BATCH, CIN, H, WIDTH), 1.0, 6.0, ((1, 16), (2, 32)))
    pre_act = noise(arg_keys[1], (BATCH, C, OH, OW), 1.0, 6.0, ((1, 16), (2, 32)))
    cotangent = noise_with(arg_keys[2], (BATCH, C, OH, OW), 1.0, 6.0, ((1, 16), (2, 32)), (2, 1, 32, 2.75))
    w_strided = noise(arg_keys[3], (4, 4, CIN, C), (16 * CIN) ** -0.5, 0.09375, ((2, 16),))
    w_square = noise(arg_keys[4], (3, 3, C, C), (9 * C) ** -0.5, 0.09375, ((2, 16),))
    return dict(features=features, pre_act=pre_act, cotangent=cotangent, w_strided=w_strided, w_square=w_square)


def reference(features, pre_act, cotangent, w_strided, w_square):
    batch_size = features.shape[0]
    out_rows = cotangent.shape[2]
    out_cols = cotangent.shape[3]
    grad_scale = 1.0 / math.sqrt(batch_size * out_rows * out_cols)
    active = jnp.maximum(pre_act, 0).astype(jnp.float32)
    padded = jnp.pad(cotangent.astype(jnp.float32), ((0, 0), (0, 0), (1, 1), (1, 1)))
    grad_active = jnp.zeros(pre_act.shape, jnp.float32)
    square_rows = []
    for tap_row in range(3):
        square_list = []
        for tap_col in range(3):
            window = padded[:, :, 2 - tap_row:2 - tap_row + out_rows, 2 - tap_col:2 - tap_col + out_cols]
            grad_active = grad_active + jnp.einsum('bdhw,cd->bchw', window, w_square[tap_row, tap_col].astype(jnp.float32))
            square_list.append(jnp.einsum('bchw,bdhw->cd', active, window))
        square_rows.append(jnp.stack(square_list))
    grad_w_square = jnp.stack(square_rows) * grad_scale
    grad_hidden = jnp.where(pre_act > 0, grad_active, 0.0)
    grad_hidden = lax.optimization_barrier(grad_hidden.astype(jnp.bfloat16)).astype(jnp.float32)
    hidden_pad = jnp.pad(grad_hidden, ((0, 0), (0, 0), (1, 1), (1, 1)))
    features_wide = features.astype(jnp.float32)
    strided_taps = {}
    phase_rows = []
    for row_phase in range(2):
        phase_list = []
        for col_phase in range(2):
            pixels = features_wide[:, :, row_phase::2, col_phase::2]
            phase_sum = jnp.zeros(pixels.shape, jnp.float32)
            for tap_row in ((row_phase + 1) % 2, (row_phase + 1) % 2 + 2):
                row_first = (row_phase + 3 - tap_row) // 2
                for tap_col in ((col_phase + 1) % 2, (col_phase + 1) % 2 + 2):
                    col_first = (col_phase + 3 - tap_col) // 2
                    window = hidden_pad[:, :, row_first:row_first + out_rows, col_first:col_first + out_cols]
                    phase_sum = phase_sum + jnp.einsum('bdhw,cd->bchw', window, w_strided[tap_row, tap_col].astype(jnp.float32))
                    strided_taps[tap_row, tap_col] = jnp.einsum('bchw,bdhw->cd', pixels, window)
            phase_list.append(phase_sum)
        phase_rows.append(jnp.stack(phase_list))
    phases = jnp.stack(phase_rows)
    grad_features = jnp.transpose(phases, (2, 3, 4, 0, 5, 1)).reshape(features.shape).astype(jnp.bfloat16)
    grad_w_strided = jnp.stack([jnp.stack([strided_taps[tap_row, tap_col] for tap_col in range(4)]) for tap_row in range(4)]) * grad_scale
    return (grad_features, grad_w_strided, grad_w_square)
```

```python
import functools
import math

import jax
import jax.numpy as jnp
from jax import lax
from jax.experimental import pallas as pl
from jax.experimental.pallas import tpu as pltpu
from jax.sharding import PartitionSpec as P

MESH = pl.DeviceIdType.MESH
BF16 = jnp.bfloat16
F32 = jnp.float32
ROWS = 32
N_CHAN = 16
HID = 32
CIN = 16
OW = 128
OUT_ROWS = 4
PIX = OUT_ROWS * OW
C = 512


def iota2(shape, dim):
    return lax.broadcasted_iota(jnp.int32, shape, dim)


def one_hot(shape, want):
    left, right = want(iota2(shape, 0), iota2(shape, 1))
    return jnp.where(left == right, 1.0, 0.0).astype(BF16)


def mm(a, b):
    return jnp.dot(a, b, preferred_element_type=F32)


def mm_nt(a, b):
    return lax.dot_general(a, b, (((1,), (1,)), ((), ())), preferred_element_type=F32)


def shift_right(x):
    lane = iota2(x.shape, 1)
    return jnp.where(lane == 0, 0.0, pltpu.roll(x, 1, axis=1))


def shift_left(x):
    lane = iota2(x.shape, 1)
    width = x.shape[1]
    return jnp.where(lane == width - 1, 0.0, pltpu.roll(x, width - 1, axis=1))


def square_cols(g):
    return g[HID : 2 * HID] + shift_right(g[2 * HID :]) + shift_left(g[:HID])


def strided_cols(g):
    t = [g[k * CIN : (k + 1) * CIN] for k in range(4)]
    return t[1] + shift_right(t[3]), t[2] + shift_left(t[0])


def kernel(
    feat_hbm, pre_hbm, cot_hbm, ws_hbm, wq_hbm,
    gf_hbm, gs_hbm, gq_hbm,
    feat_v, pre_v, cot_v, ws_v, wq_v,
    cotg, hidg, pre_t, ax, fx, a_sel, f_sel, ab, fb,
    ga_send, ga_recv, gf_send, gf_recv,
    q_own, q1, q1r, q2, q2r, q3, q3r,
    s_own, s1, s1r, s2, s2r, s3, s3r,
    gf_v, gs_v, gq_v,
    local_sem, gat_send, gat_recv, halo_ssem, halo_rsem, rs_ssem, rs_rsem,
):
    r, h = lax.axis_index("row"), lax.axis_index("chan")
    zh, y, core = r // 8, (r // 2) % 4, r % 2
    z, x = h // 4, h % 4
    up, down = ((r + ROWS - 1) % ROWS, h), ((r + 1) % ROWS, h)
    z_ids = [z + 1 - 2 * (z % 2), (z + 2) % 4, 3 - z]
    x_ids = [(x + 1) % 4, (x + 3) % 4, (x + 2) % 4]
    y_ids = [(y + 1) % 4, (y + 3) % 4, (y + 2) % 4]
    zh_ids = [(zh + 1) % 4, (zh + 3) % 4, (zh + 2) % 4]
    core_peer = (zh * 8 + y * 2 + (1 - core), h)
    y_peers = [(zh * 8 + p * 2 + core, h) for p in y_ids]
    zh_peers = [(p * 8 + y * 2 + core, h) for p in zh_ids]
    z_peers = [(r, p * 4 + x) for p in z_ids]
    x_peers = [(r, z * 4 + p) for p in x_ids]

    loads = [
        pltpu.make_async_copy(src, dst, local_sem.at[k])
        for k, (src, dst) in enumerate(
            [(cot_hbm, cot_v), (pre_hbm, pre_v), (feat_hbm, feat_v), (wq_hbm, wq_v), (ws_hbm, ws_v)]
        )
    ]
    for load in loads:
        load.start()
    partners = [core_peer, *y_peers, *zh_peers, *z_peers, *x_peers, up, down]
    barrier = pltpu.get_barrier_semaphore()
    for peer in partners:
        pl.semaphore_signal(barrier, inc=1, device_id=peer, device_id_type=MESH)

    sent = []

    def copy(src, dst, ssem, rsem, dev):
        return pltpu.make_async_remote_copy(
            src_ref=src, dst_ref=dst, send_sem=ssem, recv_sem=rsem, device_id=dev, device_id_type=MESH
        )

    def send(src, dst, ssem, rsem, dev):
        c = copy(src, dst, ssem, rsem, dev)
        c.start()
        sent.append(c)
        return c

    by_row = one_hot((128, 128), lambda i, j: (j, (i % HID) * OUT_ROWS + i // HID))
    loads[0].wait()
    cot_t = mm(by_row, cot_v[...]).astype(BF16)
    mine = pl.ds(pl.multiple_of(h * HID, HID), HID)
    for a in range(OUT_ROWS):
        cotg[mine, a * OW : (a + 1) * OW] = cot_t[a * HID : (a + 1) * HID]
    pl.semaphore_wait(barrier, len(partners))

    def block(buf, b):
        return buf.at[pl.ds(pl.multiple_of(b * HID, HID), HID)]

    def gather_start(buf, n):
        count = [0]

        def put(b, dev):
            ref = block(buf, b)
            send(ref, ref, gat_send.at[n, count[0]], gat_recv.at[n, b], dev)
            count[0] += 1

        def take(b):
            ref = block(buf, b)
            copy(ref, ref, gat_send.at[n, 0], gat_recv.at[n, b], (r, h)).wait_recv()

        for dev in z_peers:
            put(h, dev)
        for dev in x_peers:
            put(h, dev)
        return put, take

    def gather_forward(put, take):
        for p in z_ids:
            take(p * 4 + x)
            for dev in x_peers:
                put(p * 4 + x, dev)

    def gather_finish(take):
        for zz in [z, *z_ids]:
            for xx in x_ids:
                take(zz * 4 + xx)

    put, take = gather_start(cotg, 0)

    loads[1].wait()
    pre_rows = mm(by_row, pre_v[...]).astype(BF16)
    pre_t[...] = pre_rows
    ax[HID : HID + 128] = jnp.maximum(pre_rows, 0)
    halo = [
        send(ax.at[pl.ds(HID, HID)], ax.at[pl.ds(HID + 128, HID)], halo_ssem.at[0], halo_rsem.at[0], up),
        send(ax.at[pl.ds(128, HID)], ax.at[pl.ds(0, HID)], halo_ssem.at[1], halo_rsem.at[1], down),
    ]
    loads[2].wait()
    f_by_row = one_hot((128, 128), lambda i, j: (j, (i % CIN) * 8 + i // CIN))
    fx[CIN : CIN + 128] = mm(f_by_row, feat_v[...]).astype(BF16)
    halo += [
        send(fx.at[pl.ds(CIN, CIN)], fx.at[pl.ds(CIN + 128, CIN)], halo_ssem.at[2], halo_rsem.at[2], up),
        send(fx.at[pl.ds(128, CIN)], fx.at[pl.ds(0, CIN)], halo_ssem.at[3], halo_rsem.at[3], down),
    ]
    gather_forward(put, take)

    for c in halo:
        c.wait_recv()
    first, last = r == 0, r == ROWS - 1
    shifts = one_hot((OW, 3 * OW), lambda i, j: (i, j % OW + j // OW - 1))
    a_sel[...] = mm(ax[...], shifts).astype(BF16)
    strides = one_hot((2 * OW, 4 * OW), lambda i, j: (i, 2 * (j % OW) + j // OW - 1))
    f_sel[...] = mm(fx[...], strides).astype(BF16)
    a_sel[:HID] = jnp.where(first, 0.0, a_sel[:HID].astype(F32)).astype(BF16)
    a_sel[HID + 128 :] = jnp.where(last, 0.0, a_sel[HID + 128 :].astype(F32)).astype(BF16)
    f_sel[:CIN] = jnp.where(first, 0.0, f_sel[:CIN].astype(F32)).astype(BF16)
    f_sel[CIN + 128 :] = jnp.where(last, 0.0, f_sel[CIN + 128 :].astype(F32)).astype(BF16)
    for ky in range(3):
        for kx in range(3):
            t = ky * 3 + kx
            for p in range(OUT_ROWS):
                ab[t * HID : (t + 1) * HID, p * OW : (p + 1) * OW] = a_sel[
                    (p + ky) * HID : (p + ky + 1) * HID, kx * OW : (kx + 1) * OW
                ]
    for ky in range(4):
        for kx in range(4):
            t = ky * 4 + kx
            for p in range(OUT_ROWS):
                fb[t * CIN : (t + 1) * CIN, p * OW : (p + 1) * OW] = f_sel[
                    (2 * p + ky) * CIN : (2 * p + ky + 1) * CIN, kx * OW : (kx + 1) * OW
                ]
    loads[3].wait()
    loads[4].wait()
    gather_finish(take)

    ga_send[0] = square_cols(mm(wq_v[: 3 * HID], cotg[:, :OW]))
    ga_send[1] = square_cols(mm(wq_v[6 * HID :], cotg[:, PIX - OW :]))
    ga_halo = [
        send(ga_send.at[0], ga_recv.at[0], halo_ssem.at[4], halo_rsem.at[4], up),
        send(ga_send.at[1], ga_recv.at[1], halo_ssem.at[5], halo_rsem.at[5], down),
    ]
    g = mm(wq_v[...], cotg[...])
    rows = [None] * OUT_ROWS
    for ky in range(3):
        for a in range(OUT_ROWS):
            p = a + ky - 1
            if 0 <= p < OUT_ROWS:
                term = square_cols(g[ky * 3 * HID : (ky + 1) * 3 * HID, a * OW : (a + 1) * OW])
                rows[p] = term if rows[p] is None else rows[p] + term
    for c in ga_halo:
        c.wait_recv()
    rows[0] = rows[0] + jnp.where(first, 0.0, ga_recv[1])
    rows[3] = rows[3] + jnp.where(last, 0.0, ga_recv[0])
    for p in range(OUT_ROWS):
        gate = pre_t[p * HID : (p + 1) * HID].astype(F32) > 0
        hidg[mine, p * OW : (p + 1) * OW] = jnp.where(gate, rows[p], 0.0).astype(BF16)
    put, take = gather_start(hidg, 1)

    scale = 1.0 / math.sqrt(128 * 128)

    def spread(full, own, wire):
        for zz in range(4):
            for yy in range(4):
                for cc in range(2):
                    src = (zz * 8 + yy * 2 + cc) * 16
                    dst = (cc * 16 + yy * 4 + zz) * 16
                    part = full[src : src + 16]
                    own[dst : dst + 16] = part
                    wire[dst : dst + 16] = part.astype(BF16)

    def step_core(wire, got, n):
        part = wire.at[pl.ds(pl.multiple_of((1 - core) * 256, 256), 256)]
        return [send(part, got, rs_ssem.at[n, 0], rs_rsem.at[n, 0], core_peer)]

    def step_y(cs, own, got, wire, got2, n):
        for c in cs:
            c.wait_recv()
        half = pl.ds(pl.multiple_of(core * 256, 256), 256)
        total = own[half] + got[...].astype(F32)
        own[:256] = total
        wire[...] = total.astype(BF16)
        return [
            send(wire.at[pl.ds(pl.multiple_of(p * 64, 64), 64)], got2.at[k], rs_ssem.at[n, 1 + k], rs_rsem.at[n, 1 + k], dev)
            for k, (p, dev) in enumerate(zip(y_ids, y_peers))
        ]

    def step_z(cs, own, got2, wire, got3, n):
        for c in cs:
            c.wait_recv()
        total = own[pl.ds(pl.multiple_of(y * 64, 64), 64)]
        for k in range(3):
            total = total + got2[k].astype(F32)
        own[:64] = total
        wire[...] = total.astype(BF16)
        return [
            send(wire.at[pl.ds(pl.multiple_of(p * 16, 16), 16)], got3.at[k], rs_ssem.at[n, 4 + k], rs_rsem.at[n, 4 + k], dev)
            for k, (p, dev) in enumerate(zip(zh_ids, zh_peers))
        ]

    def step_end(cs, own, got3):
        for c in cs:
            c.wait_recv()
        total = own[pl.ds(pl.multiple_of(zh * 16, 16), 16)]
        for k in range(3):
            total = total + got3[k].astype(F32)
        return total * scale

    spread(mm_nt(cotg[...], ab[...]), q_own, q1)
    q_cs = step_core(q1, q1r, 0)
    gather_forward(put, take)
    q_cs = step_y(q_cs, q_own, q1r, q2, q2r, 0)
    gather_finish(take)

    spread(mm_nt(hidg[...], fb[...]), s_own, s1)
    s_cs = step_core(s1, s1r, 1)
    for n, (lo, col) in enumerate(((0, 0), (12 * CIN, PIX - OW))):
        a, b = strided_cols(mm(ws_v[lo : lo + 4 * CIN], hidg[:, col : col + OW]))
        gf_send[n, :CIN] = a
        gf_send[n, CIN:] = b
    gf_halo = [
        send(gf_send.at[0], gf_recv.at[0], halo_ssem.at[6], halo_rsem.at[6], up),
        send(gf_send.at[1], gf_recv.at[1], halo_ssem.at[7], halo_rsem.at[7], down),
    ]
    g = mm(ws_v[...], hidg[...])
    s_cs = step_y(s_cs, s_own, s1r, s2, s2r, 1)
    q_cs = step_z(q_cs, q_own, q2r, q3, q3r, 0)

    def taps(ky, i):
        return strided_cols(g[ky * 4 * CIN : (ky + 1) * 4 * CIN, i * OW : (i + 1) * OW])

    parts = []
    for f in range(8):
        u = f // 2
        if f % 2 == 0:
            near, far = taps(1, u), (taps(3, u - 1) if u else None)
        else:
            near, far = taps(2, u), (taps(0, u + 1) if u < 3 else None)
        parts.append((near, far))
    for c in gf_halo:
        c.wait_recv()
    above = jnp.where(first, 0.0, gf_recv[1])
    below = jnp.where(last, 0.0, gf_recv[0])
    lines = []
    for f, (near, far) in enumerate(parts):
        if far is None:
            edge = above if f == 0 else below
            far = (edge[:CIN], edge[CIN:])
        lines.append(jnp.concatenate([near[0] + far[0], near[1] + far[1]], axis=1).astype(BF16))
    phased = jnp.concatenate(lines, axis=0)
    weave = one_hot((2 * OW, 2 * OW), lambda i, j: (j, 2 * (i % OW) + i // OW))
    by_channel = one_hot((128, 128), lambda i, j: (j, (i % 8) * CIN + i // 8))
    woven = mm(phased, weave).astype(BF16)
    gf_v[...] = mm(by_channel, woven).astype(BF16)
    out_gf = pltpu.make_async_copy(gf_v, gf_hbm, local_sem.at[5])
    out_gf.start()

    s_cs = step_z(s_cs, s_own, s2r, s3, s3r, 1)
    gq = step_end(q_cs, q_own, q3r)
    for t in range(9):
        gq_v[t] = gq[:, t * HID : (t + 1) * HID]
    out_gq = pltpu.make_async_copy(gq_v, gq_hbm, local_sem.at[6])
    out_gq.start()
    gs_v[...] = step_end(s_cs, s_own, s3r)
    out_gs = pltpu.make_async_copy(gs_v, gs_hbm, local_sem.at[7])
    out_gs.start()
    for c in sent:
        c.wait_send()
    out_gf.wait()
    out_gq.wait()
    out_gs.wait()


def body(features, pre_act, cotangent, w_strided, w_square):
    nq, ns = 9 * HID, 16 * CIN
    any_spec = pl.BlockSpec(memory_space=pl.ANY)
    vm = pltpu.VMEM
    scratch = [
        vm((128, 256), BF16), vm((128, 128), BF16), vm((128, 128), BF16), vm((ns, C), BF16), vm((nq, C), BF16),
        vm((C, PIX), BF16), vm((C, PIX), BF16), vm((128, 128), BF16), vm((192, 128), BF16), vm((160, 256), BF16),
        vm((192, 384), BF16), vm((160, 512), BF16), vm((nq, PIX), BF16), vm((ns, PIX), BF16),
        vm((2, 32, 128), F32), vm((2, 32, 128), F32), vm((2, 32, 128), F32), vm((2, 32, 128), F32),
    ]
    for n in (nq, ns):
        scratch += [
            vm((C, n), F32), vm((C, n), BF16), vm((256, n), BF16), vm((256, n), BF16), vm((3, 64, n), BF16),
            vm((64, n), BF16), vm((3, 16, n), BF16),
        ]
    scratch += [vm((128, 256), BF16), vm((16, ns), F32), vm((9, 16, HID), F32)]
    dma = pltpu.SemaphoreType.DMA
    scratch += [dma((8,)), dma((2, 15)), dma((2, N_CHAN)), dma((8,)), dma((8,)), dma((2, 7)), dma((2, 7))]
    gf, gs, gq = pl.pallas_call(
        kernel,
        out_shape=(
            jax.ShapeDtypeStruct((128, 256), BF16),
            jax.ShapeDtypeStruct((16, ns), F32),
            jax.ShapeDtypeStruct((9, 16, HID), F32),
        ),
        in_specs=[any_spec] * 5,
        out_specs=[any_spec] * 3,
        scratch_shapes=scratch,
        compiler_params=pltpu.CompilerParams(
            collective_id=0, has_side_effects=True, vmem_limit_bytes=40 * 2**20
        ),
        name="backward",
    )(
        features.reshape(128, 256),
        pre_act.reshape(128, 128),
        cotangent.reshape(128, 128),
        w_strided.reshape(ns, C),
        w_square.reshape(nq, C),
    )
    grad_features = gf.reshape(features.shape)
    strided = jnp.transpose(gs.reshape(16, 4, 4, CIN), (1, 2, 3, 0))
    square = jnp.transpose(gq.reshape(3, 3, 16, HID), (0, 1, 3, 2))
    return grad_features, strided, square


def solution(mesh):
    in_specs = (
        P(None, "chan", "row", None),
        P(None, "chan", "row", None),
        P(None, "chan", "row", None),
        P(None, None, "chan", None),
        P(None, None, "chan", None),
    )
    out_specs = (
        P(None, "chan", "row", None),
        P(None, None, "chan", "row"),
        P(None, None, "chan", "row"),
    )
    return jax.shard_map(body, mesh=mesh, in_specs=in_specs, out_specs=out_specs, check_vma=False)
```

```python
import functools
import math

import jax
import jax.numpy as jnp
from jax import lax
from jax.experimental import pallas as pl
from jax.experimental.pallas import tpu as pltpu
from jax.sharding import PartitionSpec as P

MESH = pl.DeviceIdType.MESH
BF16 = jnp.bfloat16
F32 = jnp.float32
ROWS = 32
N_CHAN = 16
HID = 32
CIN = 16
OW = 128
OUT_ROWS = 4
PIX = OUT_ROWS * OW
C = 512


def iota2(shape, dim):
    return lax.broadcasted_iota(jnp.int32, shape, dim)


def one_hot(shape, want):
    left, right = want(iota2(shape, 0), iota2(shape, 1))
    return jnp.where(left == right, 1.0, 0.0).astype(BF16)


def mm(a, b):
    return jnp.dot(a, b, preferred_element_type=F32)


def mm_nt(a, b):
    return lax.dot_general(a, b, (((1,), (1,)), ((), ())), preferred_element_type=F32)


def shift_right(x):
    lane = iota2(x.shape, 1)
    return jnp.where(lane == 0, 0.0, pltpu.roll(x, 1, axis=1))


def shift_left(x):
    lane = iota2(x.shape, 1)
    width = x.shape[1]
    return jnp.where(lane == width - 1, 0.0, pltpu.roll(x, width - 1, axis=1))


def square_cols(g):
    return g[HID : 2 * HID] + shift_right(g[2 * HID :]) + shift_left(g[:HID])


def strided_cols(g):
    t = [g[k * CIN : (k + 1) * CIN] for k in range(4)]
    return t[1] + shift_right(t[3]), t[2] + shift_left(t[0])


def kernel(
    feat_hbm, pre_hbm, cot_hbm, ws_hbm, wq_hbm,
    gf_hbm, gs_hbm, gq_hbm,
    feat_v, pre_v, cot_v, ws_v, wq_v,
    cotg, hidg, cot_t, edge, pre_t, ax, fx, a_sel, ab, fb,
    gf_send, gf_recv,
    q_own, q1, q1r, q2, q2r, q3, q3r,
    s_own, s1, s1r, s2, s2r, s3, s3r,
    gf_v, gs_v, gq_v,
    local_sem, gat_send, gat_recv, halo_ssem, halo_rsem, edge_ssem, edge_rsem, fx_ssem, fx_rsem, rs_ssem, rs_rsem,
):
    r, h = lax.axis_index("row"), lax.axis_index("chan")
    zh, y, core = r // 8, (r // 2) % 4, r % 2
    z, x = h // 4, h % 4
    up, down = ((r + ROWS - 1) % ROWS, h), ((r + 1) % ROWS, h)
    z_ids = [z + 1 - 2 * (z % 2), (z + 2) % 4, 3 - z]
    x_ids = [(x + 1) % 4, (x + 3) % 4, (x + 2) % 4]
    y_ids = [(y + 1) % 4, (y + 3) % 4, (y + 2) % 4]
    zh_ids = [(zh + 1) % 4, (zh + 3) % 4, (zh + 2) % 4]
    core_peer = (zh * 8 + y * 2 + (1 - core), h)
    y_peers = [(zh * 8 + p * 2 + core, h) for p in y_ids]
    zh_peers = [(p * 8 + y * 2 + core, h) for p in zh_ids]
    z_peers = [(r, p * 4 + x) for p in z_ids]
    x_peers = [(r, z * 4 + p) for p in x_ids]
    owner_ids = [(z + k) % 4 for k in range(4)]
    owners = [(z * 8 + y * 2 + core, p * 4 + x) for p in owner_ids]
    giver_ids = [(zh + k) % 4 for k in range(4)]
    givers = [(p * 8 + y * 2 + core, zh * 4 + x) for p in giver_ids]
    keeps = zh == z

    loads = [
        pltpu.make_async_copy(src, dst, local_sem.at[k])
        for k, (src, dst) in enumerate(
            [(cot_hbm, cot_v), (pre_hbm, pre_v), (feat_hbm, feat_v), (wq_hbm, wq_v), (ws_hbm, ws_v)]
        )
    ]
    for load in loads:
        load.start()
    edges = [((r + d) % ROWS, p * 4 + x) for d in (ROWS - 1, 1) for p in range(4)]
    next_plane = [(r, z_ids[0] * 4 + p) for p in x_ids]
    partners = [core_peer, *y_peers, *zh_peers, *z_peers, *x_peers, *next_plane, *edges, *givers[1:]]
    barrier = pltpu.get_barrier_semaphore()
    for peer in partners:
        pl.semaphore_signal(barrier, inc=1, device_id=peer, device_id_type=MESH)

    @pl.when(jnp.logical_not(keeps))
    def _():
        pl.semaphore_signal(barrier, inc=1, device_id=givers[0], device_id_type=MESH)

    sent = []

    def copy(src, dst, ssem, rsem, dev):
        return pltpu.make_async_remote_copy(
            src_ref=src, dst_ref=dst, send_sem=ssem, recv_sem=rsem, device_id=dev, device_id_type=MESH
        )

    def send(src, dst, ssem, rsem, dev):
        c = copy(src, dst, ssem, rsem, dev)
        c.start()
        sent.append(c)
        return c

    by_row = one_hot((128, 128), lambda i, j: (j, (i % HID) * OUT_ROWS + i // HID))
    loads[0].wait()
    cot_t[...] = mm(by_row, cot_v[...]).astype(BF16)
    mine = pl.ds(pl.multiple_of(h * HID, HID), HID)
    for a in range(OUT_ROWS):
        cotg[mine, a * OW : (a + 1) * OW] = cot_t[a * HID : (a + 1) * HID]
    pl.semaphore_wait(barrier, len(partners) + jnp.where(keeps, 0, 1))

    def block(buf, b):
        return buf.at[pl.ds(pl.multiple_of(b * HID, HID), HID)]

    def gather_start(buf, n):
        count = [0]

        def put(b, dev):
            ref = block(buf, b)
            send(ref, ref, gat_send.at[n, count[0]], gat_recv.at[n, b], dev)
            count[0] += 1

        def take(b):
            ref = block(buf, b)
            copy(ref, ref, gat_send.at[n, 0], gat_recv.at[n, b], (r, h)).wait_recv()

        firsts = z_peers[1:] + x_peers + [z_peers[0]] + next_plane if n == 0 else x_peers + z_peers[1:] + [z_peers[0]] + next_plane
        for dev in firsts:
            put(h, dev)
        return put, take

    def gather_forward(put, take):
        for p in z_ids[1:]:
            take(p * 4 + x)
            for dev in x_peers:
                put(p * 4 + x, dev)

    def gather_finish(take):
        take(z_ids[0] * 4 + x)
        for zz in [z, *z_ids]:
            for xx in x_ids:
                take(zz * 4 + xx)

    for n, (d, lo, side) in enumerate(((ROWS - 1, 0, 1), (1, 96, 0))):
        for k in range(4):
            p = (z + k) % 4
            send(
                cot_t.at[pl.ds(lo, HID)], edge.at[h, pl.ds(side * HID, HID)], edge_ssem.at[n * 4 + k],
                edge_rsem.at[h, side], ((r + d) % ROWS, p * 4 + x),
            )

    put, take = gather_start(cotg, 0)

    loads[1].wait()
    pre_rows = mm(by_row, pre_v[...]).astype(BF16)
    pre_t[...] = pre_rows
    ax[HID : HID + 128] = jnp.maximum(pre_rows, 0)
    halo = [
        send(ax.at[pl.ds(HID, HID)], ax.at[pl.ds(HID + 128, HID)], halo_ssem.at[0], halo_rsem.at[0], up),
        send(ax.at[pl.ds(128, HID)], ax.at[pl.ds(0, HID)], halo_ssem.at[1], halo_rsem.at[1], down),
    ]
    loads[2].wait()
    f_by_row = one_hot((128, 128), lambda i, j: (j, (i % CIN) * 8 + i // CIN))
    fx[z, CIN : CIN + 128] = mm(f_by_row, feat_v[...]).astype(BF16)
    halo += [
        send(fx.at[z, pl.ds(CIN, CIN)], fx.at[z, pl.ds(CIN + 128, CIN)], halo_ssem.at[2], halo_rsem.at[2], up),
        send(fx.at[z, pl.ds(128, CIN)], fx.at[z, pl.ds(0, CIN)], halo_ssem.at[3], halo_rsem.at[3], down),
    ]
    gather_forward(put, take)
    for k in range(4):
        b = (z + k) % 4 * 4 + x
        for side in range(2):
            ref = edge.at[b, pl.ds(side * HID, HID)]
            copy(ref, ref, edge_ssem.at[0], edge_rsem.at[b, side], (r, h)).wait_recv()
        for j, dev in enumerate(x_peers):
            send(edge.at[b], edge.at[b], edge_ssem.at[8 + 3 * k + j], edge_rsem.at[b, 2], dev)

    first, last = r == 0, r == ROWS - 1

    def masked(flag, value):
        return jnp.where(flag, 0.0, value.astype(F32)).astype(BF16)

    for c in halo:
        c.wait_recv()
    fxm = fx.at[z]
    fxm[:CIN] = masked(first, fxm[:CIN])
    fxm[CIN + 128 :] = masked(last, fxm[CIN + 128 :])
    for k, (p, dev) in enumerate(zip(z_ids, z_peers)):
        send(fxm, fxm, fx_ssem.at[k], fx_rsem.at[z], dev)

    shifts = one_hot((OW, 3 * OW), lambda i, j: (i, j % OW + j // OW - 1))
    a_sel[...] = mm(ax[...], shifts).astype(BF16)
    a_sel[:HID] = masked(first, a_sel[:HID])
    a_sel[HID + 128 :] = masked(last, a_sel[HID + 128 :])
    for ky in range(3):
        for kx in range(3):
            t = ky * 3 + kx
            for p in range(OUT_ROWS):
                ab[t * HID : (t + 1) * HID, p * OW : (p + 1) * OW] = a_sel[
                    (p + ky) * HID : (p + ky + 1) * HID, kx * OW : (kx + 1) * OW
                ]
    loads[3].wait()
    loads[4].wait()
    gather_finish(take)

    g = mm(wq_v[...], cotg[...])
    rows = [None] * OUT_ROWS
    for ky in range(3):
        for a in range(OUT_ROWS):
            p = a + ky - 1
            if 0 <= p < OUT_ROWS:
                term = square_cols(g[ky * 3 * HID : (ky + 1) * 3 * HID, a * OW : (a + 1) * OW])
                rows[p] = term if rows[p] is None else rows[p] + term
    for zz in range(4):
        for xx in x_ids:
            b = zz * 4 + xx
            copy(edge.at[b], edge.at[b], edge_ssem.at[0], edge_rsem.at[b, 2], (r, h)).wait_recv()
    above = square_cols(mm(wq_v[6 * HID :], edge[:, :HID].reshape(C, OW)))
    below = square_cols(mm(wq_v[: 3 * HID], edge[:, HID:].reshape(C, OW)))
    rows[0] = rows[0] + jnp.where(first, 0.0, above)
    rows[3] = rows[3] + jnp.where(last, 0.0, below)
    for p in range(OUT_ROWS):
        gate = pre_t[p * HID : (p + 1) * HID].astype(F32) > 0
        hidg[mine, p * OW : (p + 1) * OW] = jnp.where(gate, rows[p], 0.0).astype(BF16)
    put, take = gather_start(hidg, 1)

    scale = 1.0 / math.sqrt(128 * 128)

    def spread(full, own, wire):
        for zz in range(4):
            for yy in range(4):
                for cc in range(2):
                    src = (zz * 8 + yy * 2 + cc) * 16
                    dst = (cc * 16 + yy * 4 + zz) * 16
                    part = full[src : src + 16]
                    own[dst : dst + 16] = part
                    wire[dst : dst + 16] = part.astype(BF16)

    def step_core(wire, got, n):
        part = wire.at[pl.ds(pl.multiple_of((1 - core) * 256, 256), 256)]
        return [send(part, got, rs_ssem.at[n, 0], rs_rsem.at[n, 0], core_peer)]

    def step_y(cs, own, got, wire, got2, n):
        for c in cs:
            c.wait_recv()
        half = pl.ds(pl.multiple_of(core * 256, 256), 256)
        total = own[half] + got[...].astype(F32)
        own[:256] = total
        wire[...] = total.astype(BF16)
        return [
            send(wire.at[pl.ds(pl.multiple_of(p * 64, 64), 64)], got2.at[k], rs_ssem.at[n, 1 + k], rs_rsem.at[n, 1 + k], dev)
            for k, (p, dev) in enumerate(zip(y_ids, y_peers))
        ]

    def step_z(cs, own, got2, wire, got3, n):
        for c in cs:
            c.wait_recv()
        total = own[pl.ds(pl.multiple_of(y * 64, 64), 64)]
        for k in range(3):
            total = total + got2[k].astype(F32)
        own[:64] = total
        wire[...] = total.astype(BF16)
        return [
            send(wire.at[pl.ds(pl.multiple_of(p * 16, 16), 16)], got3.at[k], rs_ssem.at[n, 4 + k], rs_rsem.at[n, 4 + k], dev)
            for k, (p, dev) in enumerate(zip(zh_ids, zh_peers))
        ]

    def step_end(cs, own, got3):
        for c in cs:
            c.wait_recv()
        total = own[pl.ds(pl.multiple_of(zh * 16, 16), 16)]
        for k in range(3):
            total = total + got3[k].astype(F32)
        return total * scale

    spread(mm_nt(cotg[...], ab[...]), q_own, q1)
    q_cs = step_core(q1, q1r, 0)

    strides = one_hot((2 * OW, 4 * OW), lambda i, j: (i, 2 * (j % OW) + j // OW - 1))
    for zz in range(4):

        @pl.when(z != zz)
        def _():
            copy(fx.at[zz], fx.at[zz], fx_ssem.at[0], fx_rsem.at[zz], (r, h)).wait_recv()

        f_sel = mm(fx[zz], strides).astype(BF16)
        for ky in range(4):
            for kx in range(4):
                t = zz * 16 + ky * 4 + kx
                for p in range(OUT_ROWS):
                    fb[t * CIN : (t + 1) * CIN, p * OW : (p + 1) * OW] = f_sel[
                        (2 * p + ky) * CIN : (2 * p + ky + 1) * CIN, kx * OW : (kx + 1) * OW
                    ]

    q_cs = step_y(q_cs, q_own, q1r, q2, q2r, 0)

    for xx in x_ids:
        take(z * 4 + xx)
    full = mm_nt(hidg[pl.ds(pl.multiple_of(z * 128, 128), 128)], fb[...])
    for yy in range(4):
        for cc in range(2):
            part = full[yy * 32 + cc * 16 : yy * 32 + cc * 16 + 16]
            dst = cc * 64 + yy * 16
            s_own[dst : dst + 16] = part
            s1[dst : dst + 16] = part.astype(BF16)
    s_core = send(
        s1.at[pl.ds(pl.multiple_of((1 - core) * 64, 64), 64)], s1r, rs_ssem.at[1, 0], rs_rsem.at[1, 0], core_peer
    )
    gather_forward(put, take)

    s_core.wait_recv()
    total = s_own[pl.ds(pl.multiple_of(core * 64, 64), 64)] + s1r[...].astype(F32)
    s_own[:64] = total
    s2[...] = total.astype(BF16)
    s_cs = [
        send(s2.at[pl.ds(pl.multiple_of(p * 16, 16), 16)], s2r.at[k], rs_ssem.at[1, 1 + k], rs_rsem.at[1, 1 + k], dev)
        for k, (p, dev) in enumerate(zip(y_ids, y_peers))
    ]
    q_cs = step_z(q_cs, q_own, q2r, q3, q3r, 0)
    take(z_ids[0] * 4 + x)
    for zz in z_ids:
        for xx in x_ids:
            take(zz * 4 + xx)

    for n, (lo, col) in enumerate(((0, 0), (12 * CIN, PIX - OW))):
        a, b = strided_cols(mm(ws_v[lo : lo + 4 * CIN], hidg[:, col : col + OW]))
        gf_send[n, :CIN] = a
        gf_send[n, CIN:] = b
    gf_halo = [
        send(gf_send.at[0], gf_recv.at[0], halo_ssem.at[6], halo_rsem.at[6], up),
        send(gf_send.at[1], gf_recv.at[1], halo_ssem.at[7], halo_rsem.at[7], down),
    ]
    g = mm(ws_v[...], hidg[...])
    for c in s_cs:
        c.wait_recv()
    total = s_own[pl.ds(pl.multiple_of(y * 16, 16), 16)]
    for k in range(3):
        total = total + s2r[k].astype(F32)
    for p in range(4):
        s3[p] = total[:, p * 256 : (p + 1) * 256].astype(BF16)
    last_sends = [
        copy(s3.at[p], s3r.at[zh], rs_ssem.at[1, 4 + k], rs_rsem.at[1, 4 + zh], dev)
        for k, (p, dev) in enumerate(zip(owner_ids, owners))
    ]

    @pl.when(keeps)
    def _():
        s3r[zh] = s3[z]

    @pl.when(jnp.logical_not(keeps))
    def _():
        last_sends[0].start()

    for c in last_sends[1:]:
        c.start()

    def taps(ky, i):
        return strided_cols(g[ky * 4 * CIN : (ky + 1) * 4 * CIN, i * OW : (i + 1) * OW])

    parts = []
    for f in range(8):
        u = f // 2
        if f % 2 == 0:
            near, far = taps(1, u), (taps(3, u - 1) if u else None)
        else:
            near, far = taps(2, u), (taps(0, u + 1) if u < 3 else None)
        parts.append((near, far))
    for c in gf_halo:
        c.wait_recv()
    above = jnp.where(first, 0.0, gf_recv[1])
    below = jnp.where(last, 0.0, gf_recv[0])
    lines = []
    for f, (near, far) in enumerate(parts):
        if far is None:
            edge = above if f == 0 else below
            far = (edge[:CIN], edge[CIN:])
        lines.append(jnp.concatenate([near[0] + far[0], near[1] + far[1]], axis=1).astype(BF16))
    phased = jnp.concatenate(lines, axis=0)
    weave = one_hot((2 * OW, 2 * OW), lambda i, j: (j, 2 * (i % OW) + i // OW))
    by_channel = one_hot((128, 128), lambda i, j: (j, (i % 8) * CIN + i // 8))
    woven = mm(phased, weave).astype(BF16)
    gf_v[...] = mm(by_channel, woven).astype(BF16)
    out_gf = pltpu.make_async_copy(gf_v, gf_hbm, local_sem.at[5])
    out_gf.start()

    gq = step_end(q_cs, q_own, q3r)
    for t in range(9):
        gq_v[t] = gq[:, t * HID : (t + 1) * HID]
    out_gq = pltpu.make_async_copy(gq_v, gq_hbm, local_sem.at[6])
    out_gq.start()
    last_recvs = [
        copy(s3.at[0], s3r.at[p], rs_ssem.at[1, 4], rs_rsem.at[1, 4 + p], dev) for p, dev in zip(giver_ids, givers)
    ]

    @pl.when(jnp.logical_not(keeps))
    def _():
        last_recvs[0].wait_recv()

    for c in last_recvs[1:]:
        c.wait_recv()
    total = s3r[0].astype(F32)
    for p in range(1, 4):
        total = total + s3r[p].astype(F32)
    gs_v[...] = total * scale
    out_gs = pltpu.make_async_copy(gs_v, gs_hbm, local_sem.at[7])
    out_gs.start()
    @pl.when(jnp.logical_not(keeps))
    def _():
        last_sends[0].wait_send()

    for c in sent + last_sends[1:]:
        c.wait_send()
    out_gf.wait()
    out_gq.wait()
    out_gs.wait()


def body(features, pre_act, cotangent, w_strided, w_square):
    nq, ns = 9 * HID, 16 * CIN
    any_spec = pl.BlockSpec(memory_space=pl.ANY)
    hbm = lambda v: pltpu.with_memory_space_constraint(v, pltpu.HBM)
    vm = pltpu.VMEM
    scratch = [
        vm((128, 256), BF16), vm((128, 128), BF16), vm((128, 128), BF16), vm((ns, C), BF16), vm((nq, C), BF16),
        vm((C, PIX), BF16), vm((C, PIX), BF16), vm((128, 128), BF16), vm((16, 64, 128), BF16), vm((128, 128), BF16),
        vm((192, 128), BF16), vm((4, 160, 256), BF16), vm((192, 384), BF16), vm((nq, PIX), BF16), vm((4 * ns, PIX), BF16),
        vm((2, 32, 128), F32), vm((2, 32, 128), F32),
        vm((C, nq), F32), vm((C, nq), BF16), vm((256, nq), BF16), vm((256, nq), BF16), vm((3, 64, nq), BF16),
        vm((64, nq), BF16), vm((3, 16, nq), BF16),
        vm((128, 1024), F32), vm((128, 1024), BF16), vm((64, 1024), BF16), vm((64, 1024), BF16),
        vm((3, 16, 1024), BF16), vm((4, 16, 256), BF16), vm((4, 16, 256), BF16),
    ]
    scratch += [vm((128, 256), BF16), vm((16, ns), F32), vm((9, 16, HID), F32)]
    dma = pltpu.SemaphoreType.DMA
    scratch += [dma((8,)), dma((2, 15)), dma((2, N_CHAN)), dma((8,)), dma((8,)), dma((20,)), dma((16, 3)), dma((3,)), dma((4,))]
    scratch += [dma((2, 8)), dma((2, 8))]
    gf, gs, gq = pl.pallas_call(
        kernel,
        out_shape=(
            jax.ShapeDtypeStruct((128, 256), BF16),
            jax.ShapeDtypeStruct((16, ns), F32),
            jax.ShapeDtypeStruct((9, 16, HID), F32),
        ),
        in_specs=[any_spec] * 5,
        out_specs=[any_spec] * 3,
        scratch_shapes=scratch,
        compiler_params=pltpu.CompilerParams(
            collective_id=0, has_side_effects=True, vmem_limit_bytes=40 * 2**20
        ),
        name="backward",
    )(
        hbm(features.reshape(128, 256)),
        hbm(pre_act.reshape(128, 128)),
        hbm(cotangent.reshape(128, 128)),
        hbm(w_strided.reshape(ns, C)),
        hbm(w_square.reshape(nq, C)),
    )
    grad_features = gf.reshape(features.shape)
    strided = jnp.transpose(gs.reshape(16, 4, 4, CIN), (1, 2, 3, 0))
    square = jnp.transpose(gq.reshape(3, 3, 16, HID), (0, 1, 3, 2))
    return grad_features, strided, square


def solution(mesh):
    in_specs = (
        P(None, "chan", "row", None),
        P(None, "chan", "row", None),
        P(None, "chan", "row", None),
        P(None, None, "chan", None),
        P(None, None, "chan", None),
    )
    out_specs = (
        P(None, "chan", "row", None),
        P(None, None, "chan", "row"),
        P(None, None, "chan", "row"),
    )
    return jax.shard_map(body, mesh=mesh, in_specs=in_specs, out_specs=out_specs, check_vma=False)
```

```python
import functools
import math

import jax
import jax.numpy as jnp
from jax import lax
from jax.experimental import pallas as pl
from jax.experimental.pallas import tpu as pltpu
from jax.sharding import PartitionSpec as P

MESH = pl.DeviceIdType.MESH
BF16 = jnp.bfloat16
F32 = jnp.float32
ROWS = 32
N_CHAN = 16
HID = 32
CIN = 16
OW = 128
OUT_ROWS = 4
PIX = OUT_ROWS * OW
C = 512


def iota2(shape, dim):
    return lax.broadcasted_iota(jnp.int32, shape, dim)


def one_hot(shape, want):
    left, right = want(iota2(shape, 0), iota2(shape, 1))
    return jnp.where(left == right, 1.0, 0.0).astype(BF16)


def mm(a, b):
    return jnp.dot(a, b, preferred_element_type=F32)


def mm_nt(a, b):
    return lax.dot_general(a, b, (((1,), (1,)), ((), ())), preferred_element_type=F32)


def shift_right(x):
    lane = iota2(x.shape, 1)
    return jnp.where(lane == 0, 0.0, pltpu.roll(x, 1, axis=1))


def shift_left(x):
    lane = iota2(x.shape, 1)
    width = x.shape[1]
    return jnp.where(lane == width - 1, 0.0, pltpu.roll(x, width - 1, axis=1))


def square_cols(g):
    return g[HID : 2 * HID] + shift_right(g[2 * HID :]) + shift_left(g[:HID])


def strided_cols(g):
    t = [g[k * CIN : (k + 1) * CIN] for k in range(4)]
    return t[1] + shift_right(t[3]), t[2] + shift_left(t[0])


def kernel(
    feat_hbm, pre_hbm, cot_hbm, ws_hbm, wq_hbm,
    gf_v, gs_v, gq_v,
    feat_v, pre_v, cot_v, ws_v, wq_v,
    cotg, hidg, cot_t, edge, pre_t, ax, fx, a_sel, ab, fb,
    gf_send, gf_recv,
    q_own, q1, q1r, q2, q2r, q3, q3r,
    s_own, s1, s1r, s2, s2r, s3, s3r,
    local_sem, gat_send, gat_recv, halo_ssem, halo_rsem, edge_ssem, edge_rsem, fx_ssem, fx_rsem, rs_ssem, rs_rsem,
):
    r, h = lax.axis_index("row"), lax.axis_index("chan")
    zh, y, core = r // 8, (r // 2) % 4, r % 2
    z, x = h // 4, h % 4
    up, down = ((r + ROWS - 1) % ROWS, h), ((r + 1) % ROWS, h)
    z_ids = [z + 1 - 2 * (z % 2), (z + 2) % 4, 3 - z]
    x_ids = [(x + 1) % 4, (x + 3) % 4, (x + 2) % 4]
    y_ids = [(y + 1) % 4, (y + 3) % 4, (y + 2) % 4]
    zh_ids = [(zh + 1) % 4, (zh + 3) % 4, (zh + 2) % 4]
    core_peer = (zh * 8 + y * 2 + (1 - core), h)
    y_peers = [(zh * 8 + p * 2 + core, h) for p in y_ids]
    zh_peers = [(p * 8 + y * 2 + core, h) for p in zh_ids]
    z_peers = [(r, p * 4 + x) for p in z_ids]
    x_peers = [(r, z * 4 + p) for p in x_ids]
    owner_ids = [(z + k) % 4 for k in range(4)]
    owners = [(z * 8 + y * 2 + core, p * 4 + x) for p in owner_ids]
    giver_ids = [(zh + k) % 4 for k in range(4)]
    givers = [(p * 8 + y * 2 + core, zh * 4 + x) for p in giver_ids]
    keeps = zh == z

    loads = [
        pltpu.make_async_copy(src, dst, local_sem.at[k])
        for k, (src, dst) in enumerate(
            [(cot_hbm, cot_v), (pre_hbm, pre_v), (feat_hbm, feat_v), (wq_hbm, wq_v), (ws_hbm, ws_v)]
        )
    ]
    for load in loads:
        load.start()
    edges = [((r + d) % ROWS, p * 4 + x) for d in (ROWS - 1, 1) for p in range(4)]
    next_plane = [(r, z_ids[0] * 4 + p) for p in x_ids]
    partners = [core_peer, *y_peers, *zh_peers, *z_peers, *x_peers, *next_plane, *edges, *givers[1:]]
    barrier = pltpu.get_barrier_semaphore()
    for peer in partners:
        pl.semaphore_signal(barrier, inc=1, device_id=peer, device_id_type=MESH)

    @pl.when(jnp.logical_not(keeps))
    def _():
        pl.semaphore_signal(barrier, inc=1, device_id=givers[0], device_id_type=MESH)

    sent = []

    def copy(src, dst, ssem, rsem, dev):
        return pltpu.make_async_remote_copy(
            src_ref=src, dst_ref=dst, send_sem=ssem, recv_sem=rsem, device_id=dev, device_id_type=MESH
        )

    def send(src, dst, ssem, rsem, dev):
        c = copy(src, dst, ssem, rsem, dev)
        c.start()
        sent.append(c)
        return c

    by_row = one_hot((128, 128), lambda i, j: (j, (i % HID) * OUT_ROWS + i // HID))
    loads[0].wait()
    cot_t[...] = mm(by_row, cot_v[...]).astype(BF16)
    mine = pl.ds(pl.multiple_of(h * HID, HID), HID)
    for a in range(OUT_ROWS):
        cotg[mine, a * OW : (a + 1) * OW] = cot_t[a * HID : (a + 1) * HID]
    pl.semaphore_wait(barrier, len(partners) + jnp.where(keeps, 0, 1))

    def block(buf, b):
        return buf.at[pl.ds(pl.multiple_of(b * HID, HID), HID)]

    def gather_start(buf, n):
        count = [0]

        def put(b, dev):
            ref = block(buf, b)
            send(ref, ref, gat_send.at[n, count[0]], gat_recv.at[n, b], dev)
            count[0] += 1

        def take(b):
            ref = block(buf, b)
            copy(ref, ref, gat_send.at[n, 0], gat_recv.at[n, b], (r, h)).wait_recv()

        firsts = z_peers[1:] + x_peers + [z_peers[0]] + next_plane if n == 0 else x_peers + z_peers[1:] + [z_peers[0]] + next_plane
        for dev in firsts:
            put(h, dev)
        return put, take

    def gather_forward(put, take):
        for p in z_ids[1:]:
            take(p * 4 + x)
            for dev in x_peers:
                put(p * 4 + x, dev)

    def gather_finish(take):
        take(z_ids[0] * 4 + x)
        for zz in [z, *z_ids]:
            for xx in x_ids:
                take(zz * 4 + xx)

    for n, (d, lo, side) in enumerate(((ROWS - 1, 0, 1), (1, 96, 0))):
        for k in range(4):
            p = (z + k) % 4
            send(
                cot_t.at[pl.ds(lo, HID)], edge.at[h, pl.ds(side * HID, HID)], edge_ssem.at[n * 4 + k],
                edge_rsem.at[h, side], ((r + d) % ROWS, p * 4 + x),
            )

    put, take = gather_start(cotg, 0)

    loads[1].wait()
    pre_rows = mm(by_row, pre_v[...]).astype(BF16)
    pre_t[...] = pre_rows
    ax[HID : HID + 128] = jnp.maximum(pre_rows, 0)
    halo = [
        send(ax.at[pl.ds(HID, HID)], ax.at[pl.ds(HID + 128, HID)], halo_ssem.at[0], halo_rsem.at[0], up),
        send(ax.at[pl.ds(128, HID)], ax.at[pl.ds(0, HID)], halo_ssem.at[1], halo_rsem.at[1], down),
    ]
    loads[2].wait()
    f_by_row = one_hot((128, 128), lambda i, j: (j, (i % CIN) * 8 + i // CIN))
    fx[z, CIN : CIN + 128] = mm(f_by_row, feat_v[...]).astype(BF16)
    halo += [
        send(fx.at[z, pl.ds(CIN, CIN)], fx.at[z, pl.ds(CIN + 128, CIN)], halo_ssem.at[2], halo_rsem.at[2], up),
        send(fx.at[z, pl.ds(128, CIN)], fx.at[z, pl.ds(0, CIN)], halo_ssem.at[3], halo_rsem.at[3], down),
    ]
    gather_forward(put, take)
    fx_rows = fx.at[z, pl.ds(CIN, 128)]
    for k, dev in enumerate(z_peers):
        send(fx_rows, fx_rows, fx_ssem.at[k], fx_rsem.at[z, 0], dev)
    for k in range(4):
        b = (z + k) % 4 * 4 + x
        for side in range(2):
            ref = edge.at[b, pl.ds(side * HID, HID)]
            copy(ref, ref, edge_ssem.at[0], edge_rsem.at[b, side], (r, h)).wait_recv()
        for j, dev in enumerate(x_peers):
            send(edge.at[b], edge.at[b], edge_ssem.at[8 + 3 * k + j], edge_rsem.at[b, 2], dev)

    first, last = r == 0, r == ROWS - 1

    def masked(flag, value):
        return jnp.where(flag, 0.0, value.astype(F32)).astype(BF16)

    for c in halo:
        c.wait_recv()
    fx[z, :CIN] = masked(first, fx[z, :CIN])
    fx[z, CIN + 128 :] = masked(last, fx[z, CIN + 128 :])
    for n, lo in enumerate((0, CIN + 128)):
        rim = fx.at[z, pl.ds(lo, CIN)]
        for k, dev in enumerate(z_peers):
            send(rim, rim, fx_ssem.at[3 + 3 * n + k], fx_rsem.at[z, 1 + n], dev)

    shifts = one_hot((OW, 3 * OW), lambda i, j: (i, j % OW + j // OW - 1))
    a_sel[...] = mm(ax[...], shifts).astype(BF16)
    a_sel[:HID] = masked(first, a_sel[:HID])
    a_sel[HID + 128 :] = masked(last, a_sel[HID + 128 :])
    for ky in range(3):
        for kx in range(3):
            t = ky * 3 + kx
            for p in range(OUT_ROWS):
                ab[t * HID : (t + 1) * HID, p * OW : (p + 1) * OW] = a_sel[
                    (p + ky) * HID : (p + ky + 1) * HID, kx * OW : (kx + 1) * OW
                ]
    loads[3].wait()
    loads[4].wait()
    gather_finish(take)

    g = mm(wq_v[...], cotg[...])
    rows = [None] * OUT_ROWS
    for ky in range(3):
        for a in range(OUT_ROWS):
            p = a + ky - 1
            if 0 <= p < OUT_ROWS:
                term = square_cols(g[ky * 3 * HID : (ky + 1) * 3 * HID, a * OW : (a + 1) * OW])
                rows[p] = term if rows[p] is None else rows[p] + term
    for zz in range(4):
        for xx in x_ids:
            b = zz * 4 + xx
            copy(edge.at[b], edge.at[b], edge_ssem.at[0], edge_rsem.at[b, 2], (r, h)).wait_recv()
    above = square_cols(mm(wq_v[6 * HID :], edge[:, :HID].reshape(C, OW)))
    below = square_cols(mm(wq_v[: 3 * HID], edge[:, HID:].reshape(C, OW)))
    rows[0] = rows[0] + jnp.where(first, 0.0, above)
    rows[3] = rows[3] + jnp.where(last, 0.0, below)
    for p in range(OUT_ROWS):
        gate = pre_t[p * HID : (p + 1) * HID].astype(F32) > 0
        hidg[mine, p * OW : (p + 1) * OW] = jnp.where(gate, rows[p], 0.0).astype(BF16)
    put, take = gather_start(hidg, 1)

    scale = 1.0 / math.sqrt(128 * 128)

    def spread(full, own, wire):
        for zz in range(4):
            for yy in range(4):
                for cc in range(2):
                    src = (zz * 8 + yy * 2 + cc) * 16
                    dst = (cc * 16 + yy * 4 + zz) * 16
                    part = full[src : src + 16]
                    own[dst : dst + 16] = part
                    wire[dst : dst + 16] = part.astype(BF16)

    def step_core(wire, got, n):
        part = wire.at[pl.ds(pl.multiple_of((1 - core) * 256, 256), 256)]
        return [send(part, got, rs_ssem.at[n, 0], rs_rsem.at[n, 0], core_peer)]

    def step_y(cs, own, got, wire, got2, n):
        for c in cs:
            c.wait_recv()
        half = pl.ds(pl.multiple_of(core * 256, 256), 256)
        total = own[half] + got[...].astype(F32)
        own[:256] = total
        wire[...] = total.astype(BF16)
        return [
            send(wire.at[pl.ds(pl.multiple_of(p * 64, 64), 64)], got2.at[k], rs_ssem.at[n, 1 + k], rs_rsem.at[n, 1 + k], dev)
            for k, (p, dev) in enumerate(zip(y_ids, y_peers))
        ]

    def step_z(cs, own, got2, wire, got3, n):
        for c in cs:
            c.wait_recv()
        total = own[pl.ds(pl.multiple_of(y * 64, 64), 64)]
        for k in range(3):
            total = total + got2[k].astype(F32)
        own[:64] = total
        wire[...] = total.astype(BF16)
        return [
            send(wire.at[pl.ds(pl.multiple_of(p * 16, 16), 16)], got3.at[k], rs_ssem.at[n, 4 + k], rs_rsem.at[n, 4 + k], dev)
            for k, (p, dev) in enumerate(zip(zh_ids, zh_peers))
        ]

    def step_end(cs, own, got3):
        for c in cs:
            c.wait_recv()
        total = own[pl.ds(pl.multiple_of(zh * 16, 16), 16)]
        for k in range(3):
            total = total + got3[k].astype(F32)
        return total * scale

    spread(mm_nt(cotg[...], ab[...]), q_own, q1)
    q_cs = step_core(q1, q1r, 0)

    strides = one_hot((2 * OW, 4 * OW), lambda i, j: (i, 2 * (j % OW) + j // OW - 1))
    for zz in range(4):

        @pl.when(z != zz)
        def _():
            for n, (lo, size) in enumerate(((CIN, 128), (0, CIN), (CIN + 128, CIN))):
                ref = fx.at[zz, pl.ds(lo, size)]
                copy(ref, ref, fx_ssem.at[0], fx_rsem.at[zz, n], (r, h)).wait_recv()

        f_sel = mm(fx[zz], strides).astype(BF16)
        for ky in range(4):
            for kx in range(4):
                t = zz * 16 + ky * 4 + kx
                for p in range(OUT_ROWS):
                    fb[t * CIN : (t + 1) * CIN, p * OW : (p + 1) * OW] = f_sel[
                        (2 * p + ky) * CIN : (2 * p + ky + 1) * CIN, kx * OW : (kx + 1) * OW
                    ]

    q_cs = step_y(q_cs, q_own, q1r, q2, q2r, 0)

    for xx in x_ids:
        take(z * 4 + xx)
    full = mm_nt(hidg[pl.ds(pl.multiple_of(z * 128, 128), 128)], fb[...])
    for yy in range(4):
        for cc in range(2):
            part = full[yy * 32 + cc * 16 : yy * 32 + cc * 16 + 16]
            dst = cc * 64 + yy * 16
            s_own[dst : dst + 16] = part
            s1[dst : dst + 16] = part.astype(BF16)
    s_core = send(
        s1.at[pl.ds(pl.multiple_of((1 - core) * 64, 64), 64)], s1r, rs_ssem.at[1, 0], rs_rsem.at[1, 0], core_peer
    )
    gather_forward(put, take)

    s_core.wait_recv()
    total = s_own[pl.ds(pl.multiple_of(core * 64, 64), 64)] + s1r[...].astype(F32)
    s_own[:64] = total
    s2[...] = total.astype(BF16)
    s_cs = [
        send(s2.at[pl.ds(pl.multiple_of(p * 16, 16), 16)], s2r.at[k], rs_ssem.at[1, 1 + k], rs_rsem.at[1, 1 + k], dev)
        for k, (p, dev) in enumerate(zip(y_ids, y_peers))
    ]
    q_cs = step_z(q_cs, q_own, q2r, q3, q3r, 0)
    take(z_ids[0] * 4 + x)
    for zz in z_ids:
        for xx in x_ids:
            take(zz * 4 + xx)

    for n, (lo, col) in enumerate(((0, 0), (12 * CIN, PIX - OW))):
        a, b = strided_cols(mm(ws_v[lo : lo + 4 * CIN], hidg[:, col : col + OW]))
        gf_send[n, :CIN] = a
        gf_send[n, CIN:] = b
    gf_halo = [
        send(gf_send.at[0], gf_recv.at[0], halo_ssem.at[6], halo_rsem.at[6], up),
        send(gf_send.at[1], gf_recv.at[1], halo_ssem.at[7], halo_rsem.at[7], down),
    ]
    g = mm(ws_v[...], hidg[...])
    for c in s_cs:
        c.wait_recv()
    total = s_own[pl.ds(pl.multiple_of(y * 16, 16), 16)]
    for k in range(3):
        total = total + s2r[k].astype(F32)
    for p in range(4):
        s3[p] = total[:, p * 256 : (p + 1) * 256].astype(BF16)
    last_sends = [
        copy(s3.at[p], s3r.at[zh], rs_ssem.at[1, 4 + k], rs_rsem.at[1, 4 + zh], dev)
        for k, (p, dev) in enumerate(zip(owner_ids, owners))
    ]

    @pl.when(keeps)
    def _():
        s3r[zh] = s3[z]

    @pl.when(jnp.logical_not(keeps))
    def _():
        last_sends[0].start()

    for c in last_sends[1:]:
        c.start()

    def taps(ky, i):
        return strided_cols(g[ky * 4 * CIN : (ky + 1) * 4 * CIN, i * OW : (i + 1) * OW])

    parts = []
    for f in range(8):
        u = f // 2
        if f % 2 == 0:
            near, far = taps(1, u), (taps(3, u - 1) if u else None)
        else:
            near, far = taps(2, u), (taps(0, u + 1) if u < 3 else None)
        parts.append((near, far))
    for c in gf_halo:
        c.wait_recv()
    above = jnp.where(first, 0.0, gf_recv[1])
    below = jnp.where(last, 0.0, gf_recv[0])
    lines = []
    for f, (near, far) in enumerate(parts):
        if far is None:
            edge = above if f == 0 else below
            far = (edge[:CIN], edge[CIN:])
        lines.append(jnp.concatenate([near[0] + far[0], near[1] + far[1]], axis=1).astype(BF16))
    phased = jnp.concatenate(lines, axis=0)
    weave = one_hot((2 * OW, 2 * OW), lambda i, j: (j, 2 * (i % OW) + i // OW))
    by_channel = one_hot((128, 128), lambda i, j: (j, (i % 8) * CIN + i // 8))
    woven = mm(phased, weave).astype(BF16)
    gf_v[...] = mm(by_channel, woven).astype(BF16)

    gq = step_end(q_cs, q_own, q3r)
    for t in range(9):
        gq_v[t] = gq[:, t * HID : (t + 1) * HID]
    last_recvs = [
        copy(s3.at[0], s3r.at[p], rs_ssem.at[1, 4], rs_rsem.at[1, 4 + p], dev) for p, dev in zip(giver_ids, givers)
    ]

    @pl.when(jnp.logical_not(keeps))
    def _():
        last_recvs[0].wait_recv()

    for c in last_recvs[1:]:
        c.wait_recv()
    total = s3r[0].astype(F32)
    for p in range(1, 4):
        total = total + s3r[p].astype(F32)
    gs_v[...] = (total * scale).T
    @pl.when(jnp.logical_not(keeps))
    def _():
        last_sends[0].wait_send()

    for c in sent + last_sends[1:]:
        c.wait_send()


def body(features, pre_act, cotangent, w_strided, w_square):
    nq, ns = 9 * HID, 16 * CIN
    any_spec = pl.BlockSpec(memory_space=pl.ANY)
    hbm = lambda v: pltpu.with_memory_space_constraint(v, pltpu.HBM)
    vm = pltpu.VMEM
    scratch = [
        vm((128, 256), BF16), vm((128, 128), BF16), vm((128, 128), BF16), vm((ns, C), BF16), vm((nq, C), BF16),
        vm((C, PIX), BF16), vm((C, PIX), BF16), vm((128, 128), BF16), vm((16, 64, 128), BF16), vm((128, 128), BF16),
        vm((192, 128), BF16), vm((4, 160, 256), BF16), vm((192, 384), BF16), vm((nq, PIX), BF16), vm((4 * ns, PIX), BF16),
        vm((2, 32, 128), F32), vm((2, 32, 128), F32),
        vm((C, nq), F32), vm((C, nq), BF16), vm((256, nq), BF16), vm((256, nq), BF16), vm((3, 64, nq), BF16),
        vm((64, nq), BF16), vm((3, 16, nq), BF16),
        vm((128, 1024), F32), vm((128, 1024), BF16), vm((64, 1024), BF16), vm((64, 1024), BF16),
        vm((3, 16, 1024), BF16), vm((4, 16, 256), BF16), vm((4, 16, 256), BF16),
    ]
    dma = pltpu.SemaphoreType.DMA
    scratch += [dma((8,)), dma((2, 15)), dma((2, N_CHAN)), dma((8,)), dma((8,)), dma((20,)), dma((16, 3)), dma((9,)), dma((4, 3))]
    scratch += [dma((2, 8)), dma((2, 8))]
    gf, gs, gq = pl.pallas_call(
        kernel,
        out_shape=(
            jax.ShapeDtypeStruct((128, 256), BF16),
            jax.ShapeDtypeStruct((ns, 16), F32),
            jax.ShapeDtypeStruct((9, 16, HID), F32),
        ),
        in_specs=[any_spec] * 5,
        out_specs=[pl.BlockSpec(memory_space=pltpu.VMEM)] * 3,
        scratch_shapes=scratch,
        compiler_params=pltpu.CompilerParams(
            collective_id=0, has_side_effects=True, vmem_limit_bytes=40 * 2**20
        ),
        name="backward",
    )(
        hbm(features.reshape(128, 256)),
        hbm(pre_act.reshape(128, 128)),
        hbm(cotangent.reshape(128, 128)),
        hbm(w_strided.reshape(ns, C)),
        hbm(w_square.reshape(nq, C)),
    )
    grad_features = gf.reshape(features.shape)
    strided = gs.reshape(4, 4, CIN, 16)
    square = jnp.transpose(gq.reshape(3, 3, 16, HID), (0, 1, 3, 2))
    return grad_features, strided, square


def solution(mesh):
    in_specs = (
        P(None, "chan", "row", None),
        P(None, "chan", "row", None),
        P(None, "chan", "row", None),
        P(None, None, "chan", None),
        P(None, None, "chan", None),
    )
    out_specs = (
        P(None, "chan", "row", None),
        P(None, None, "chan", "row"),
        P(None, None, "chan", "row"),
    )
    return jax.shard_map(body, mesh=mesh, in_specs=in_specs, out_specs=out_specs, check_vma=False)
```

```python
import functools
import math

import jax
import jax.numpy as jnp
from jax import lax
from jax.experimental import pallas as pl
from jax.experimental.pallas import tpu as pltpu
from jax.sharding import PartitionSpec as P

MESH = pl.DeviceIdType.MESH
BF16 = jnp.bfloat16
F32 = jnp.float32
ROWS = 32
N_CHAN = 16
HID = 32
CIN = 16
OW = 128
OUT_ROWS = 4
PIX = OUT_ROWS * OW
C = 512


def iota2(shape, dim):
    return lax.broadcasted_iota(jnp.int32, shape, dim)


def one_hot(shape, want):
    left, right = want(iota2(shape, 0), iota2(shape, 1))
    return jnp.where(left == right, 1.0, 0.0).astype(BF16)


def mm(a, b):
    return jnp.dot(a, b, preferred_element_type=F32)


def mm_nt(a, b):
    return lax.dot_general(a, b, (((1,), (1,)), ((), ())), preferred_element_type=F32)


def shift_right(x):
    lane = iota2(x.shape, 1)
    return jnp.where(lane == 0, 0.0, pltpu.roll(x, 1, axis=1))


def shift_left(x):
    lane = iota2(x.shape, 1)
    width = x.shape[1]
    return jnp.where(lane == width - 1, 0.0, pltpu.roll(x, width - 1, axis=1))


def square_cols(g):
    return g[HID : 2 * HID] + shift_right(g[2 * HID :]) + shift_left(g[:HID])


def strided_cols(g):
    t = [g[k * CIN : (k + 1) * CIN] for k in range(4)]
    return t[1] + shift_right(t[3]), t[2] + shift_left(t[0])


def kernel(
    feat_hbm, pre_hbm, cot_hbm, ws_hbm, wq_hbm,
    gf_v, gs_v, gq_v,
    feat_v, pre_v, cot_v, ws_v, wq_v,
    cotg, hidg, cot_t, edge, pre_t, ax, fx, a_sel, ab, fb,
    gf_send, gf_recv,
    q_own, q1, q1r, q2, q2r, q3, q3r,
    s_own, s1, s1r, s2, s2r, s3, s3r,
    local_sem, gat_send, gat_recv, halo_ssem, halo_rsem, edge_ssem, edge_rsem, fx_ssem, fx_rsem, rs_ssem, rs_rsem,
):
    r, h = lax.axis_index("row"), lax.axis_index("chan")
    zh, y, core = r // 8, (r // 2) % 4, r % 2
    z, x = h // 4, h % 4
    up, down = ((r + ROWS - 1) % ROWS, h), ((r + 1) % ROWS, h)
    z_ids = [z + 1 - 2 * (z % 2), (z + 2) % 4, 3 - z]
    x_ids = [(x + 1) % 4, (x + 3) % 4, (x + 2) % 4]
    y_ids = [(y + 1) % 4, (y + 3) % 4, (y + 2) % 4]
    zh_ids = [(zh + 1) % 4, (zh + 3) % 4, (zh + 2) % 4]
    core_peer = (zh * 8 + y * 2 + (1 - core), h)
    y_peers = [(zh * 8 + p * 2 + core, h) for p in y_ids]
    zh_peers = [(p * 8 + y * 2 + core, h) for p in zh_ids]
    z_peers = [(r, p * 4 + x) for p in z_ids]
    x_peers = [(r, z * 4 + p) for p in x_ids]
    owner_ids = [(z + k) % 4 for k in range(4)]
    owners = [(z * 8 + y * 2 + core, p * 4 + x) for p in owner_ids]
    giver_ids = [(zh + k) % 4 for k in range(4)]
    givers = [(p * 8 + y * 2 + core, zh * 4 + x) for p in giver_ids]
    keeps = zh == z

    loads = [
        pltpu.make_async_copy(src, dst, local_sem.at[k])
        for k, (src, dst) in enumerate(
            [(cot_hbm, cot_v), (pre_hbm, pre_v), (feat_hbm, feat_v), (wq_hbm, wq_v), (ws_hbm, ws_v)]
        )
    ]
    for load in loads:
        load.start()
    edges = [((r + d) % ROWS, p * 4 + x) for d in (ROWS - 1, 1) for p in range(4)]
    next_plane = [(r, z_ids[0] * 4 + p) for p in x_ids]
    partners = [core_peer, *y_peers, *zh_peers, *z_peers, *x_peers, *next_plane, *edges, *givers[1:]]
    barrier = pltpu.get_barrier_semaphore()
    for peer in partners:
        pl.semaphore_signal(barrier, inc=1, device_id=peer, device_id_type=MESH)

    @pl.when(jnp.logical_not(keeps))
    def _():
        pl.semaphore_signal(barrier, inc=1, device_id=givers[0], device_id_type=MESH)

    sent = []

    def copy(src, dst, ssem, rsem, dev):
        return pltpu.make_async_remote_copy(
            src_ref=src, dst_ref=dst, send_sem=ssem, recv_sem=rsem, device_id=dev, device_id_type=MESH
        )

    def send(src, dst, ssem, rsem, dev):
        c = copy(src, dst, ssem, rsem, dev)
        c.start()
        sent.append(c)
        return c

    by_row = one_hot((128, 128), lambda i, j: (j, (i % HID) * OUT_ROWS + i // HID))
    loads[0].wait()
    cot_t[...] = mm(by_row, cot_v[...]).astype(BF16)
    mine = pl.ds(pl.multiple_of(h * HID, HID), HID)
    for a in range(OUT_ROWS):
        cotg[mine, a * OW : (a + 1) * OW] = cot_t[a * HID : (a + 1) * HID]
    pl.semaphore_wait(barrier, len(partners) + jnp.where(keeps, 0, 1))

    def block(buf, b):
        return buf.at[pl.ds(pl.multiple_of(b * HID, HID), HID)]

    def gather_start(buf, n):
        count = [0]

        def put(b, dev):
            ref = block(buf, b)
            send(ref, ref, gat_send.at[n, count[0]], gat_recv.at[n, b], dev)
            count[0] += 1

        def take(b):
            ref = block(buf, b)
            copy(ref, ref, gat_send.at[n, 0], gat_recv.at[n, b], (r, h)).wait_recv()

        firsts = z_peers[1:] + x_peers + [z_peers[0]] + next_plane
        for dev in firsts:
            put(h, dev)
        return put, take

    def gather_forward(put, take):
        for p in z_ids[1:]:
            take(p * 4 + x)
            for dev in x_peers:
                put(p * 4 + x, dev)

    def gather_finish(take):
        take(z_ids[0] * 4 + x)
        for zz in [z, *z_ids]:
            for xx in x_ids:
                take(zz * 4 + xx)

    for n, (d, lo, side) in enumerate(((ROWS - 1, 0, 1), (1, 96, 0))):
        for k in range(4):
            p = (z + k) % 4
            send(
                cot_t.at[pl.ds(lo, HID)], edge.at[h, pl.ds(side * HID, HID)], edge_ssem.at[n * 4 + k],
                edge_rsem.at[h, side], ((r + d) % ROWS, p * 4 + x),
            )

    put, take = gather_start(cotg, 0)

    loads[1].wait()
    pre_rows = mm(by_row, pre_v[...]).astype(BF16)
    pre_t[...] = pre_rows
    ax[HID : HID + 128] = jnp.maximum(pre_rows, 0)
    halo = [
        send(ax.at[pl.ds(HID, HID)], ax.at[pl.ds(HID + 128, HID)], halo_ssem.at[0], halo_rsem.at[0], up),
        send(ax.at[pl.ds(128, HID)], ax.at[pl.ds(0, HID)], halo_ssem.at[1], halo_rsem.at[1], down),
    ]
    loads[2].wait()
    f_by_row = one_hot((128, 128), lambda i, j: (j, (i % CIN) * 8 + i // CIN))
    fx[z, CIN : CIN + 128] = mm(f_by_row, feat_v[...]).astype(BF16)
    halo += [
        send(fx.at[z, pl.ds(CIN, CIN)], fx.at[z, pl.ds(CIN + 128, CIN)], halo_ssem.at[2], halo_rsem.at[2], up),
        send(fx.at[z, pl.ds(128, CIN)], fx.at[z, pl.ds(0, CIN)], halo_ssem.at[3], halo_rsem.at[3], down),
    ]
    gather_forward(put, take)
    fx_rows = fx.at[z, pl.ds(CIN, 128)]
    for k, dev in enumerate(z_peers):
        send(fx_rows, fx_rows, fx_ssem.at[k], fx_rsem.at[z, 0], dev)
    for k in range(4):
        b = (z + k) % 4 * 4 + x
        for side in range(2):
            ref = edge.at[b, pl.ds(side * HID, HID)]
            copy(ref, ref, edge_ssem.at[0], edge_rsem.at[b, side], (r, h)).wait_recv()
        for j, dev in enumerate(x_peers):
            send(edge.at[b], edge.at[b], edge_ssem.at[8 + 3 * k + j], edge_rsem.at[b, 2], dev)

    first, last = r == 0, r == ROWS - 1

    def masked(flag, value):
        return jnp.where(flag, 0.0, value.astype(F32)).astype(BF16)

    for c in halo:
        c.wait_recv()
    fx[z, :CIN] = masked(first, fx[z, :CIN])
    fx[z, CIN + 128 :] = masked(last, fx[z, CIN + 128 :])
    for n, lo in enumerate((0, CIN + 128)):
        rim = fx.at[z, pl.ds(lo, CIN)]
        for k, dev in enumerate(z_peers):
            send(rim, rim, fx_ssem.at[3 + 3 * n + k], fx_rsem.at[z, 1 + n], dev)

    shifts = one_hot((OW, 3 * OW), lambda i, j: (i, j % OW + j // OW - 1))
    a_sel[...] = mm(ax[...], shifts).astype(BF16)
    a_sel[:HID] = masked(first, a_sel[:HID])
    a_sel[HID + 128 :] = masked(last, a_sel[HID + 128 :])
    for ky in range(3):
        for kx in range(3):
            t = ky * 3 + kx
            for p in range(OUT_ROWS):
                ab[t * HID : (t + 1) * HID, p * OW : (p + 1) * OW] = a_sel[
                    (p + ky) * HID : (p + ky + 1) * HID, kx * OW : (kx + 1) * OW
                ]
    loads[3].wait()
    loads[4].wait()
    gather_finish(take)

    g = mm(wq_v[...], cotg[...])
    rows = [None] * OUT_ROWS
    for ky in range(3):
        for a in range(OUT_ROWS):
            p = a + ky - 1
            if 0 <= p < OUT_ROWS:
                term = square_cols(g[ky * 3 * HID : (ky + 1) * 3 * HID, a * OW : (a + 1) * OW])
                rows[p] = term if rows[p] is None else rows[p] + term
    for zz in range(4):
        for xx in x_ids:
            b = zz * 4 + xx
            copy(edge.at[b], edge.at[b], edge_ssem.at[0], edge_rsem.at[b, 2], (r, h)).wait_recv()
    above = square_cols(mm(wq_v[6 * HID :], edge[:, :HID].reshape(C, OW)))
    below = square_cols(mm(wq_v[: 3 * HID], edge[:, HID:].reshape(C, OW)))
    rows[0] = rows[0] + jnp.where(first, 0.0, above)
    rows[3] = rows[3] + jnp.where(last, 0.0, below)
    for p in range(OUT_ROWS):
        gate = pre_t[p * HID : (p + 1) * HID].astype(F32) > 0
        hidg[mine, p * OW : (p + 1) * OW] = jnp.where(gate, rows[p], 0.0).astype(BF16)
    put, take = gather_start(hidg, 1)

    scale = 1.0 / math.sqrt(128 * 128)

    def spread(full, own, wire):
        for zz in range(4):
            for yy in range(4):
                for cc in range(2):
                    src = (zz * 8 + yy * 2 + cc) * 16
                    dst = (cc * 16 + yy * 4 + zz) * 16
                    part = full[src : src + 16]
                    own[dst : dst + 16] = part
                    wire[dst : dst + 16] = part.astype(BF16)

    def step_core(wire, got, n):
        part = wire.at[pl.ds(pl.multiple_of((1 - core) * 256, 256), 256)]
        return [send(part, got, rs_ssem.at[n, 0], rs_rsem.at[n, 0], core_peer)]

    def step_y(cs, own, got, wire, got2, n):
        for c in cs:
            c.wait_recv()
        half = pl.ds(pl.multiple_of(core * 256, 256), 256)
        total = own[half] + got[...].astype(F32)
        own[:256] = total
        wire[...] = total.astype(BF16)
        return [
            send(wire.at[pl.ds(pl.multiple_of(p * 64, 64), 64)], got2.at[k], rs_ssem.at[n, 1 + k], rs_rsem.at[n, 1 + k], dev)
            for k, (p, dev) in enumerate(zip(y_ids, y_peers))
        ]

    def step_z(cs, own, got2, wire, got3, n):
        for c in cs:
            c.wait_recv()
        total = own[pl.ds(pl.multiple_of(y * 64, 64), 64)]
        for k in range(3):
            total = total + got2[k].astype(F32)
        own[:64] = total
        wire[...] = total.astype(BF16)
        return [
            send(wire.at[pl.ds(pl.multiple_of(p * 16, 16), 16)], got3.at[k], rs_ssem.at[n, 4 + k], rs_rsem.at[n, 4 + k], dev)
            for k, (p, dev) in enumerate(zip(zh_ids, zh_peers))
        ]

    def step_end(cs, own, got3):
        for c in cs:
            c.wait_recv()
        total = own[pl.ds(pl.multiple_of(zh * 16, 16), 16)]
        for k in range(3):
            total = total + got3[k].astype(F32)
        return total * scale

    spread(mm_nt(cotg[...], ab[...]), q_own, q1)
    q_cs = step_core(q1, q1r, 0)

    strides = one_hot((2 * OW, 4 * OW), lambda i, j: (i, 2 * (j % OW) + j // OW - 1))
    for zz in range(4):

        @pl.when(z != zz)
        def _():
            for n, (lo, size) in enumerate(((CIN, 128), (0, CIN), (CIN + 128, CIN))):
                ref = fx.at[zz, pl.ds(lo, size)]
                copy(ref, ref, fx_ssem.at[0], fx_rsem.at[zz, n], (r, h)).wait_recv()

        f_sel = mm(fx[zz], strides).astype(BF16)
        for ky in range(4):
            for kx in range(4):
                t = zz * 16 + ky * 4 + kx
                for p in range(OUT_ROWS):
                    fb[t * CIN : (t + 1) * CIN, p * OW : (p + 1) * OW] = f_sel[
                        (2 * p + ky) * CIN : (2 * p + ky + 1) * CIN, kx * OW : (kx + 1) * OW
                    ]

    q_cs = step_y(q_cs, q_own, q1r, q2, q2r, 0)

    for xx in x_ids:
        take(z * 4 + xx)
    full = mm_nt(hidg[pl.ds(pl.multiple_of(z * 128, 128), 128)], fb[...])
    for yy in range(4):
        for cc in range(2):
            part = full[yy * 32 + cc * 16 : yy * 32 + cc * 16 + 16]
            dst = cc * 64 + yy * 16
            s_own[dst : dst + 16] = part
            s1[dst : dst + 16] = part.astype(BF16)
    s_core = send(
        s1.at[pl.ds(pl.multiple_of((1 - core) * 64, 64), 64)], s1r, rs_ssem.at[1, 0], rs_rsem.at[1, 0], core_peer
    )
    gather_forward(put, take)

    s_core.wait_recv()
    total = s_own[pl.ds(pl.multiple_of(core * 64, 64), 64)] + s1r[...].astype(F32)
    s_own[:64] = total
    s2[...] = total.astype(BF16)
    s_cs = [
        send(s2.at[pl.ds(pl.multiple_of(p * 16, 16), 16)], s2r.at[k], rs_ssem.at[1, 1 + k], rs_rsem.at[1, 1 + k], dev)
        for k, (p, dev) in enumerate(zip(y_ids, y_peers))
    ]
    q_cs = step_z(q_cs, q_own, q2r, q3, q3r, 0)
    take(z_ids[0] * 4 + x)
    for zz in z_ids:
        for xx in x_ids:
            take(zz * 4 + xx)

    for n, (lo, col) in enumerate(((0, 0), (12 * CIN, PIX - OW))):
        a, b = strided_cols(mm(ws_v[lo : lo + 4 * CIN], hidg[:, col : col + OW]))
        gf_send[n, :CIN] = a
        gf_send[n, CIN:] = b
    gf_halo = [
        send(gf_send.at[0], gf_recv.at[0], halo_ssem.at[6], halo_rsem.at[6], up),
        send(gf_send.at[1], gf_recv.at[1], halo_ssem.at[7], halo_rsem.at[7], down),
    ]
    g = mm(ws_v[...], hidg[...])
    for c in s_cs:
        c.wait_recv()
    total = s_own[pl.ds(pl.multiple_of(y * 16, 16), 16)]
    for k in range(3):
        total = total + s2r[k].astype(F32)
    for p in range(4):
        s3[p] = total[:, p * 256 : (p + 1) * 256].astype(BF16)
    last_sends = [
        copy(s3.at[p], s3r.at[zh], rs_ssem.at[1, 4 + k], rs_rsem.at[1, 4 + zh], dev)
        for k, (p, dev) in enumerate(zip(owner_ids, owners))
    ]

    @pl.when(keeps)
    def _():
        s3r[zh] = s3[z]

    @pl.when(jnp.logical_not(keeps))
    def _():
        last_sends[0].start()

    for c in last_sends[1:]:
        c.start()

    def taps(ky, i):
        return strided_cols(g[ky * 4 * CIN : (ky + 1) * 4 * CIN, i * OW : (i + 1) * OW])

    parts = []
    for f in range(8):
        u = f // 2
        if f % 2 == 0:
            near, far = taps(1, u), (taps(3, u - 1) if u else None)
        else:
            near, far = taps(2, u), (taps(0, u + 1) if u < 3 else None)
        parts.append((near, far))
    for c in gf_halo:
        c.wait_recv()
    above = jnp.where(first, 0.0, gf_recv[1])
    below = jnp.where(last, 0.0, gf_recv[0])
    lines = []
    for f, (near, far) in enumerate(parts):
        if far is None:
            edge = above if f == 0 else below
            far = (edge[:CIN], edge[CIN:])
        lines.append(jnp.concatenate([near[0] + far[0], near[1] + far[1]], axis=1).astype(BF16))
    phased = jnp.concatenate(lines, axis=0)
    weave = one_hot((2 * OW, 2 * OW), lambda i, j: (j, 2 * (i % OW) + i // OW))
    by_channel = one_hot((128, 128), lambda i, j: (j, (i % 8) * CIN + i // 8))
    woven = mm(phased, weave).astype(BF16)
    gf_v[...] = mm(by_channel, woven).astype(BF16)

    gq = step_end(q_cs, q_own, q3r)
    for t in range(9):
        gq_v[t] = gq[:, t * HID : (t + 1) * HID]
    last_recvs = [
        copy(s3.at[0], s3r.at[p], rs_ssem.at[1, 4], rs_rsem.at[1, 4 + p], dev) for p, dev in zip(giver_ids, givers)
    ]

    @pl.when(jnp.logical_not(keeps))
    def _():
        last_recvs[0].wait_recv()

    for c in last_recvs[1:]:
        c.wait_recv()
    total = s3r[0].astype(F32)
    for p in range(1, 4):
        total = total + s3r[p].astype(F32)
    gs_v[...] = (total * scale).T
    @pl.when(jnp.logical_not(keeps))
    def _():
        last_sends[0].wait_send()

    for c in sent + last_sends[1:]:
        c.wait_send()


def body(features, pre_act, cotangent, w_strided, w_square):
    nq, ns = 9 * HID, 16 * CIN
    any_spec = pl.BlockSpec(memory_space=pl.ANY)
    hbm = lambda v: pltpu.with_memory_space_constraint(v, pltpu.HBM)
    vm = pltpu.VMEM
    scratch = [
        vm((128, 256), BF16), vm((128, 128), BF16), vm((128, 128), BF16), vm((ns, C), BF16), vm((nq, C), BF16),
        vm((C, PIX), BF16), vm((C, PIX), BF16), vm((128, 128), BF16), vm((16, 64, 128), BF16), vm((128, 128), BF16),
        vm((192, 128), BF16), vm((4, 160, 256), BF16), vm((192, 384), BF16), vm((nq, PIX), BF16), vm((4 * ns, PIX), BF16),
        vm((2, 32, 128), F32), vm((2, 32, 128), F32),
        vm((C, nq), F32), vm((C, nq), BF16), vm((256, nq), BF16), vm((256, nq), BF16), vm((3, 64, nq), BF16),
        vm((64, nq), BF16), vm((3, 16, nq), BF16),
        vm((128, 1024), F32), vm((128, 1024), BF16), vm((64, 1024), BF16), vm((64, 1024), BF16),
        vm((3, 16, 1024), BF16), vm((4, 16, 256), BF16), vm((4, 16, 256), BF16),
    ]
    dma = pltpu.SemaphoreType.DMA
    scratch += [dma((8,)), dma((2, 15)), dma((2, N_CHAN)), dma((8,)), dma((8,)), dma((20,)), dma((16, 3)), dma((9,)), dma((4, 3))]
    scratch += [dma((2, 8)), dma((2, 8))]
    gf, gs, gq = pl.pallas_call(
        kernel,
        out_shape=(
            jax.ShapeDtypeStruct((128, 256), BF16),
            jax.ShapeDtypeStruct((ns, 16), F32),
            jax.ShapeDtypeStruct((9, 16, HID), F32),
        ),
        in_specs=[any_spec] * 5,
        out_specs=[pl.BlockSpec(memory_space=pltpu.VMEM)] * 3,
        scratch_shapes=scratch,
        compiler_params=pltpu.CompilerParams(
            collective_id=0, has_side_effects=True, vmem_limit_bytes=40 * 2**20
        ),
        name="backward",
    )(
        hbm(features.reshape(128, 256)),
        hbm(pre_act.reshape(128, 128)),
        hbm(cotangent.reshape(128, 128)),
        hbm(w_strided.reshape(ns, C)),
        hbm(w_square.reshape(nq, C)),
    )
    grad_features = gf.reshape(features.shape)
    strided = gs.reshape(4, 4, CIN, 16)
    square = jnp.transpose(gq.reshape(3, 3, 16, HID), (0, 1, 3, 2))
    return grad_features, strided, square


def solution(mesh):
    in_specs = (
        P(None, "chan", "row", None),
        P(None, "chan", "row", None),
        P(None, "chan", "row", None),
        P(None, None, "chan", None),
        P(None, None, "chan", None),
    )
    out_specs = (
        P(None, "chan", "row", None),
        P(None, None, "chan", "row"),
        P(None, None, "chan", "row"),
    )
    return jax.shard_map(body, mesh=mesh, in_specs=in_specs, out_specs=out_specs, check_vma=False)
```
